32 devices in a mesh: dp: 2 (over x), row: 4 (over z), col: 4 (over y, core).
Axes of the slice: x: 2, y: 2, z: 4, core: 2. Of those that a mesh axis runs over, the one named last changes fastest.
Arguments:
- activations: bfloat16 [512, 7424], P('col', ('dp', 'row')), may hold values from -6 to 6
- upstream: bfloat16 [512, 29696], P(('dp', 'row'), 'col'), may hold values from -0.375 to 0.375
- weight: bfloat16 [7424, 29696], P(('dp', 'row'), 'col'), may hold values from -0.75 to 0.75
- bin_fill: int32 [8], P(('dp', 'row')), may hold values from 16 to 64, as said below
Outputs:
- d_input: bfloat16 [512, 7424], P('col', ('dp', 'row'))
- d_weight: bfloat16 [7424, 29696], P(('dp', 'row'), 'col')
The draws below stay inside these ranges and needn't reach their ends.
Inputs may be any that keep to these rules, and one draw needn't show every extreme that they name: `bin_fill`: in every draw some bin is full, with 64 tokens, and some bin holds 16 tokens.
All inputs are finite; a program needn't handle non-finite values.
Results may differ from the reference program's by a relative error of at most 0.001.
Values may be sent and summed in bfloat16 or wider, within the bound.
A program may use at most 64 MiB of HBM per device.

```python
import jax
import jax.numpy as jnp

D = 7424
FF = 29696
TOKENS = 512
BIN_LEN = 64
BINS = 8


def draw_bin_fill(key, part):
    key = jax.random.fold_in(key, 11)
    first_key, second_key = jax.random.split(key)
    lowest = max(BIN_LEN // 4, 1)
    fills = jax.random.randint(first_key, (BINS,), lowest, BIN_LEN + 1)
    chosen = jax.random.randint(second_key, (), 0, BINS)
    places = jnp.arange(BINS, dtype=jnp.int32)
    fills = jnp.where(places == chosen, BIN_LEN, fills)
    fills = jnp.where(places == (chosen + 1) % BINS, lowest, fills)
    return fills.astype(jnp.int32)


def strengthened(array, key, source, target, parts, factor):
    def block_of(dim):
        return (jnp.arange(array.shape[dim]) // (array.shape[dim] // parts)).reshape((-1,) + (1,) * (array.ndim - 1 - dim))

    near = jax.random.permutation(key, parts)[block_of(target)]
    other_side = (block_of(target) + parts // 2) % parts
    return jnp.where((block_of(source) == near) | (block_of(source) == other_side), factor * array, array)


def block_levels(own_key, dims, pieces, low, top_value):
    def one(position, shards_of):
        steps = jax.random.uniform(jax.random.fold_in(jax.random.fold_in(own_key, 6), position), (shards_of,), jnp.float32, low / len(pieces), top_value / len(pieces))
        return jnp.repeat(jnp.exp(steps), dims[position] // shards_of).reshape((-1,) + (1,) * (len(dims) - position - 1))

    factor_of = one(*pieces[0])
    for cut in pieces[1:]:
        factor_of = factor_of * one(*cut)
    return factor_of


def scatter_about(own_key, extent, spread, limit, cuts=(), held_as=jnp.bfloat16):
    array = jax.random.normal(own_key, extent, jnp.float32) * spread
    if len(cuts) > 0:
        array = block_levels(own_key, extent, cuts, -0.22, 0.18) * array
    return jnp.clip(array, min=-limit, max=limit).astype(held_as)


def bell_draw_with(own_key, dims, deviation, reach, cuts, heavy, held_as=jnp.bfloat16):
    entries = deviation * jax.random.normal(own_key, dims, jnp.float32)
    if cuts:
        entries = entries * block_levels(own_key, dims, cuts, -0.22, 0.18)
    return jnp.clip(strengthened(entries, jax.random.fold_in(own_key, 3), *heavy), -reach, reach).astype(held_as)


def setup_inputs(seed: int = 0) -> dict:
    streams_of = jax.random.split(jax.random.key(seed), 5)
    activations = scatter_about(streams_of[0], (TOKENS, D), 1.0, 6.0, ((0, 4), (1, 8)))
    upstream = bell_draw_with(streams_of[1], (TOKENS, FF), (TOKENS ** -0.5), 0.375, ((0, 8), (1, 4)), (1, 0, 8, 2.0))
    weight = scatter_about(streams_of[2], (D, FF), (max(FF // TOKENS, 1)) ** -0.5, 0.75, ((0, 8), (1, 4)))
    bin_fill = draw_bin_fill(jax.random.fold_in(streams_of[4], 71), 0)
    return {"activations": activations, "upstream": upstream, "weight": weight, "bin_fill": bin_fill}


def reference(activations, upstream, weight, bin_fill):
    slot_index = jnp.arange(TOKENS, dtype=jnp.int32) % BIN_LEN
    owner_bin = jnp.arange(TOKENS, dtype=jnp.int32) // BIN_LEN
    live_rows = slot_index < bin_fill[owner_bin]
    masked = jnp.where(live_rows[:, None], upstream, jnp.zeros_like(upstream))
    d_input = jnp.dot(masked, weight.T, preferred_element_type=jnp.float32).astype(jnp.bfloat16)
    d_weight = jnp.dot(activations.T, masked, preferred_element_type=jnp.float32).astype(jnp.bfloat16)
    return d_input, d_weight
```

```python
import functools

import jax
import jax.numpy as jnp
from jax import lax
from jax.experimental import pallas as pl
from jax.experimental.pallas import tpu as pltpu
from jax.sharding import PartitionSpec as P

MESH = pl.DeviceIdType.MESH
ROWS = 16
STEPS = 14


def own(plane, order=(0, 1, 2, 3)):
    return [(plane, 0, quarter) for quarter in order]


def other(plane, order=(0, 1, 2, 3)):
    return [(plane, 1, quarter) for quarter in order]


END = {
    "x": own(0) + own(1) + own(2) + own(3, (0, 1)),
    "in": own(0) + other(0),
}
MIDDLE = {
    "x": own(1) + own(2) + own(3, (2, 3, 0, 1)),
    "in": own(1) + own(0),
    "out": own(1) + own(2) + own(3) + other(3, (2, 3)),
}
LINKS = ("x", "in", "out")
ORDER = ((0, 1, 2, 3), (1, 0, 2, 3))


def gather_kernel(
    up_ref, fill_ref, act_ref, w_ref, g_out, act_t_out, din_out,
    gv, wv, av, acc, parts, piece_in, piece_out, act_in, act_sent,
    part_in, part_sent, w_sem, g_sem,
):
    x, z, c = lax.axis_index("dp"), lax.axis_index("row"), lax.axis_index("col")
    side = z // 2
    is_end = (z == 0) | (z == 3)
    is_middle = (z == 1) | (z == 2)
    inward, outward = z + 1 - 2 * side, z - 1 + 2 * side
    targets = {"x": {"dp": 1 - x}, "in": {"row": inward}, "out": {"row": outward}}
    peers = [{"col": lax.rem(c + k, 4)} for k in (1, 2, 3)]
    ff = gv.shape[2]
    tiles = ff // 256

    def absolute(plane):
        return plane + side * (3 - 2 * plane)

    load_w = pltpu.make_async_copy(w_ref, wv, w_sem)
    load_w.start()
    live = lax.broadcasted_iota(jnp.int32, up_ref.shape, 0) < fill_ref[0]
    here = pl.ds(pl.multiple_of(x * 64, 64), 64)
    gv[z, here, :] = jnp.where(live, up_ref[...], jnp.zeros_like(up_ref))
    av[c] = act_ref[...]

    barrier = pltpu.get_barrier_semaphore()
    for target in [targets["x"], targets["in"]] + peers:
        pl.semaphore_signal(barrier, inc=1, device_id=target, device_id_type=MESH)

    @pl.when(is_middle)
    def _():
        pl.semaphore_signal(barrier, inc=1, device_id=targets["out"], device_id_type=MESH)
        pl.semaphore_wait(barrier, 6)

    @pl.when(is_end)
    def _():
        pl.semaphore_wait(barrier, 5)

    def piece_copy(piece, link, step):
        plane, from_other, quarter = piece
        xs = 1 - x if from_other else x
        rows = pl.ds(pl.multiple_of(xs * 64 + quarter * ROWS, ROWS), ROWS)
        ref = gv.at[absolute(plane), rows, :]
        return pltpu.make_async_remote_copy(
            src_ref=ref, dst_ref=ref,
            send_sem=piece_out.at[LINKS.index(link), step],
            recv_sem=piece_in.at[absolute(plane), xs * 4 + quarter],
            device_id=targets[link], device_id_type=MESH,
        )

    arrived = [set(own(0)), set(own(1))]

    def need(role, piece):
        if piece not in arrived[role]:
            arrived[role].add(piece)
            piece_copy(piece, "x", 0).wait_recv()

    def send_step(role, step):
        queues = (END, MIDDLE)[role]
        for link, queue in queues.items():
            if 2 <= step < len(queue) + 2:
                piece_copy(queue[step - 2], link, step - 2).wait_send()
            if step < len(queue):
                need(role, queue[step])
                piece_copy(queue[step], link, step).start()

    def each_role(do):
        pl.when(is_end)(lambda: do(0))
        pl.when(is_middle)(lambda: do(1))

    def lump_plane(lump):
        first, second = ORDER[0][lump], ORDER[1][lump]
        return absolute(jnp.where(is_end, first, second))

    def bin_copy(plane, xs):
        return pltpu.make_async_copy(
            gv.at[plane, pl.ds(xs * 64, 64), :],
            g_out.at[pl.ds(pl.multiple_of((xs * 4 + plane) * 64, 64), 64), :],
            g_sem.at[plane, xs],
        )

    def prepare(lump):
        def wait_all(role):
            plane = ORDER[role][lump]
            for piece in own(plane) + other(plane):
                need(role, piece)

        each_role(wait_all)
        plane = lump_plane(lump)
        for xs in range(2):
            bin_copy(plane, xs).start()
        acc[plane] = jnp.zeros_like(acc[plane])

    def multiply(lump, low, high):
        plane = lump_plane(lump)

        def body(k, carry):
            cols = pl.ds(pl.multiple_of(k * 256, 256), 256)
            acc[plane] += lax.dot_general(
                gv[plane, :, cols], wv[:, cols], (((1,), (1,)), ((), ())),
                preferred_element_type=jnp.float32,
            )
            return carry

        lax.fori_loop(low, high, body, 0)

    def part_copy(plane, xs):
        owner = xs * 2 + plane // 2
        apart = lax.rem(c - owner + 4, 4)
        slot = jnp.maximum(apart - 1, 0)
        copy = pltpu.make_async_remote_copy(
            src_ref=acc.at[plane, pl.ds(xs * 64, 64), :],
            dst_ref=parts.at[slot, lax.rem(plane, 2)],
            send_sem=part_sent.at[plane, xs],
            recv_sem=part_in.at[slot, lax.rem(plane, 2)],
            device_id={"col": owner}, device_id_type=MESH,
        )
        return apart != 0, copy

    def send_parts(lump):
        for xs in range(2):
            remote, copy = part_copy(lump_plane(lump), xs)
            pl.when(remote)(copy.start)

    def act_copy(k):
        return pltpu.make_async_remote_copy(
            src_ref=av.at[c], dst_ref=av.at[c],
            send_sem=act_sent.at[k], recv_sem=act_in.at[k],
            device_id=peers[k], device_id_type=MESH,
        )

    cut = [0] + [(tiles * i) // 4 for i in (1, 2, 3)] + [tiles]
    for step in range(STEPS):
        each_role(functools.partial(lambda step, role: send_step(role, step), step))
        if step == 0:
            for k in range(3):
                act_copy(k).start()
        if step == 3:
            for k in range(3):
                act_copy(k).wait()
            for k in range(4):
                act_t_out[:, k * 128:(k + 1) * 128] = av[k].T
            load_w.wait()
        if step in (5, 9, 13):
            prepare((step - 5) // 4)
        if 5 <= step < 13:
            lump, slice_of = (step - 5) // 4, (step - 5) % 4
            multiply(lump, cut[slice_of], cut[slice_of + 1])
            if slice_of == 3:
                send_parts(lump)
        if step == 13:
            multiply(2, 0, cut[2])
    multiply(2, cut[2], tiles)
    send_parts(2)
    prepare(3)
    multiply(3, 0, tiles)
    send_parts(3)
    for step in (STEPS, STEPS + 1):
        each_role(functools.partial(lambda step, role: send_step(role, step), step))
    for par in range(2):
        plane = 2 * lax.rem(c, 2) + par
        total = acc[plane, pl.ds(pl.multiple_of((c // 2) * 64, 64), 64), :]
        for k in range(3):
            pltpu.make_async_remote_copy(
                src_ref=parts.at[k, par], dst_ref=parts.at[k, par],
                send_sem=part_sent.at[0, 0], recv_sem=part_in.at[k, par],
                device_id=peers[k], device_id_type=MESH,
            ).wait_recv()
            total += parts[k, par]
        din_out[par * 64:(par + 1) * 64, :] = total.astype(din_out.dtype)
    for plane in range(4):
        for xs in range(2):
            remote, copy = part_copy(plane, xs)
            pl.when(remote)(copy.wait_send)
            bin_copy(plane, xs).wait()


def weight_kernel(act_ref, g_ref, out_ref):
    for k in range(g_ref.shape[1] // 256):
        cols = slice(k * 256, (k + 1) * 256)
        out_ref[:, cols] = jnp.dot(
            act_ref[...], g_ref[:, cols], preferred_element_type=jnp.float32
        ).astype(out_ref.dtype)


def fused(activations, upstream, weight, bin_fill):
    d, ff = weight.shape
    tokens = upstream.shape[0] * 8
    vmem = pl.BlockSpec(memory_space=pltpu.VMEM)
    hbm = pl.BlockSpec(memory_space=pl.ANY)
    dma = pltpu.SemaphoreType.DMA
    bf16, f32 = jnp.bfloat16, jnp.float32
    gathered, act_t, d_input = pl.pallas_call(
        gather_kernel,
        out_shape=(
            jax.ShapeDtypeStruct((tokens, ff), bf16),
            jax.ShapeDtypeStruct((d, tokens), bf16),
            jax.ShapeDtypeStruct((128, d), bf16),
        ),
        in_specs=[vmem, pl.BlockSpec(memory_space=pltpu.SMEM), vmem, hbm],
        out_specs=(hbm, vmem, vmem),
        scratch_shapes=[
            pltpu.VMEM((4, 128, ff), bf16),
            pltpu.VMEM((d, ff), bf16),
            pltpu.VMEM((4, 128, d), bf16),
            pltpu.VMEM((4, 128, d), f32),
            pltpu.VMEM((3, 2, 64, d), f32),
            dma((4, 8)), dma((3, STEPS)), dma((3,)), dma((3,)),
            dma((3, 2)), dma((4, 2)), dma, dma((4, 2)),
        ],
        compiler_params=pltpu.CompilerParams(
            collective_id=0, has_side_effects=True, vmem_limit_bytes=44 * 2**20
        ),
        cost_estimate=pl.CostEstimate(
            flops=2 * tokens * ff * d, bytes_accessed=2 * ff * (d + tokens), transcendentals=0
        ),
    )(upstream, bin_fill, activations, weight)
    tile = 1024
    d_weight = pl.pallas_call(
        weight_kernel,
        out_shape=jax.ShapeDtypeStruct((d, ff), bf16),
        grid=(pl.cdiv(ff, tile),),
        in_specs=[
            pl.BlockSpec((d, tokens), lambda i: (0, 0)),
            pl.BlockSpec((tokens, tile), lambda i: (0, i)),
        ],
        out_specs=pl.BlockSpec((d, tile), lambda i: (0, i)),
        compiler_params=pltpu.CompilerParams(vmem_limit_bytes=40 * 2**20),
        cost_estimate=pl.CostEstimate(
            flops=2 * tokens * ff * d, bytes_accessed=2 * ff * (d + tokens), transcendentals=0
        ),
    )(act_t, gathered)
    return d_input, d_weight


def plain(activations, upstream, weight, bin_fill):
    live_rows = jnp.arange(upstream.shape[0], dtype=jnp.int32) < bin_fill[0]
    masked = jnp.where(live_rows[:, None], upstream, jnp.zeros_like(upstream))
    all_inputs = lax.all_gather(activations, "col", axis=0, tiled=True)
    block_rows = lax.all_gather(masked, ("dp", "row"), axis=0, tiled=True)
    grad_w = lax.dot_general(
        all_inputs, block_rows, (((0,), (0,)), ((), ())), preferred_element_type=jnp.float32
    )
    grad_x = lax.dot_general(
        block_rows, weight, (((1,), (1,)), ((), ())), preferred_element_type=jnp.float32
    )
    d_input = lax.psum_scatter(grad_x, "col", scatter_dimension=0, tiled=True)
    return d_input.astype(jnp.bfloat16), grad_w.astype(jnp.bfloat16)


def solution(mesh):
    sizes = tuple(mesh.shape[name] for name in ("dp", "row", "col"))
    in_specs = (
        P("col", ("dp", "row")),
        P(("dp", "row"), "col"),
        P(("dp", "row"), "col"),
        P(("dp", "row")),
    )
    out_specs = (P("col", ("dp", "row")), P(("dp", "row"), "col"))
    return jax.shard_map(
        fused if sizes == (2, 4, 4) else plain,
        mesh=mesh, in_specs=in_specs, out_specs=out_specs, check_vma=False,
    )
```

```python
import functools

import jax
import jax.numpy as jnp
from jax import lax
from jax.experimental import pallas as pl
from jax.experimental.pallas import tpu as pltpu
from jax.sharding import PartitionSpec as P

MESH = pl.DeviceIdType.MESH
PIECES = 4
STEPS = 14


def own(plane, order=(0, 1, 2, 3)):
    return [(plane, 0, quarter) for quarter in order]


def other(plane, order=(0, 1, 2, 3)):
    return [(plane, 1, quarter) for quarter in order]


END = {
    "x": own(0) + own(1) + own(2) + own(3, (0, 1)),
    "in": own(0) + other(0),
}
MIDDLE = {
    "x": own(1) + own(2) + own(3, (2, 3, 0, 1)),
    "in": own(1) + own(0),
    "out": own(1) + own(2) + own(3) + other(3, (2, 3)),
}
LINKS = ("x", "in", "out")
ORDER = ((0, 1, 2, 3), (1, 0, 2, 3))


def gather_kernel(
    up_ref, fill_ref, act_ref, w_ref, g_out, act_t_out, din_out,
    gv, wv, uv, av, acc, parts, piece_in, piece_out, act_in, act_sent,
    part_in, part_sent, w_sem, up_sem, g_sem,
):
    x, z, c = lax.axis_index("dp"), lax.axis_index("row"), lax.axis_index("col")
    side = z // 2
    is_end = (z == 0) | (z == 3)
    is_middle = (z == 1) | (z == 2)
    inward, outward = z + 1 - 2 * side, z - 1 + 2 * side
    targets = {"x": {"dp": 1 - x}, "in": {"row": inward}, "out": {"row": outward}}
    peers = [{"col": lax.rem(c + k, 4)} for k in (1, 2, 3)]
    ff = gv.shape[2]
    tiles = ff // 256
    cut = [tiles * i // PIECES for i in range(PIECES + 1)]

    def absolute(plane):
        return plane + side * (3 - 2 * plane)

    load_up = pltpu.make_async_copy(up_ref, uv, up_sem)
    load_up.start()
    load_w = pltpu.make_async_copy(w_ref, wv, w_sem)
    load_w.start()
    barrier = pltpu.get_barrier_semaphore()
    for target in [targets["x"], targets["in"]] + peers:
        pl.semaphore_signal(barrier, inc=1, device_id=target, device_id_type=MESH)

    @pl.when(is_middle)
    def _():
        pl.semaphore_signal(barrier, inc=1, device_id=targets["out"], device_id_type=MESH)

    av[c] = act_ref[...]
    load_up.wait()
    live = lax.broadcasted_iota(jnp.int32, uv.shape, 0) < fill_ref[0]
    here = pl.ds(pl.multiple_of(x * 64, 64), 64)
    gv[z, here, :] = jnp.where(live, uv[...], jnp.zeros_like(uv))

    @pl.when(is_middle)
    def _():
        pl.semaphore_wait(barrier, 6)

    @pl.when(is_end)
    def _():
        pl.semaphore_wait(barrier, 5)

    def piece_copy(piece, link, step):
        plane, from_other, chunk = piece
        xs = 1 - x if from_other else x
        rows = pl.ds(pl.multiple_of(xs * 64, 64), 64)
        low, high = cut[chunk] * 256, cut[chunk + 1] * 256
        ref = gv.at[absolute(plane), rows, low:high]
        return pltpu.make_async_remote_copy(
            src_ref=ref, dst_ref=ref,
            send_sem=piece_out.at[LINKS.index(link), step],
            recv_sem=piece_in.at[absolute(plane), xs * PIECES + chunk],
            device_id=targets[link], device_id_type=MESH,
        )

    arrived = [set(own(0)), set(own(1))]

    def need(role, piece):
        if piece not in arrived[role]:
            arrived[role].add(piece)
            piece_copy(piece, "x", 0).wait_recv()

    def send_step(role, step):
        queues = (END, MIDDLE)[role]
        for link, queue in queues.items():
            if 2 <= step < len(queue) + 2:
                piece_copy(queue[step - 2], link, step - 2).wait_send()
            if step < len(queue):
                need(role, queue[step])
                piece_copy(queue[step], link, step).start()

    def each_role(do):
        pl.when(is_end)(lambda: do(0))
        pl.when(is_middle)(lambda: do(1))

    def lump_plane(lump):
        first, second = ORDER[0][lump], ORDER[1][lump]
        return absolute(jnp.where(is_end, first, second))

    def bin_copy(plane, xs):
        return pltpu.make_async_copy(
            gv.at[plane, pl.ds(xs * 64, 64), :],
            g_out.at[pl.ds(pl.multiple_of((xs * 4 + plane) * 64, 64), 64), :],
            g_sem.at[plane, xs],
        )

    def multiply_chunk(lump, chunk):
        def wait_chunk(role):
            plane = ORDER[role][lump]
            need(role, (plane, 0, chunk))
            need(role, (plane, 1, chunk))

        each_role(wait_chunk)
        multiply(lump, cut[chunk], cut[chunk + 1])

    def save_bins(lump):
        for xs in range(2):
            bin_copy(lump_plane(lump), xs).start()

    def multiply(lump, low, high):
        plane = lump_plane(lump)

        def body(k, carry):
            cols = pl.ds(pl.multiple_of(k * 256, 256), 256)
            acc[plane] += lax.dot_general(
                gv[plane, :, cols], wv[:, cols], (((1,), (1,)), ((), ())),
                preferred_element_type=jnp.float32,
            )
            return carry

        lax.fori_loop(low, high, body, 0)

    def part_copy(plane, xs):
        owner = xs * 2 + plane // 2
        apart = lax.rem(c - owner + 4, 4)
        slot = jnp.maximum(apart - 1, 0)
        copy = pltpu.make_async_remote_copy(
            src_ref=acc.at[plane, pl.ds(xs * 64, 64), :],
            dst_ref=parts.at[slot, lax.rem(plane, 2)],
            send_sem=part_sent.at[plane, xs],
            recv_sem=part_in.at[slot, lax.rem(plane, 2)],
            device_id={"col": owner}, device_id_type=MESH,
        )
        return apart != 0, copy

    def send_parts(lump):
        for xs in range(2):
            remote, copy = part_copy(lump_plane(lump), xs)
            pl.when(remote)(copy.start)

    def act_copy(k):
        return pltpu.make_async_remote_copy(
            src_ref=av.at[c], dst_ref=av.at[c],
            send_sem=act_sent.at[k], recv_sem=act_in.at[k],
            device_id=peers[k], device_id_type=MESH,
        )

    acc[...] = jnp.zeros_like(acc)
    for step in range(STEPS):
        each_role(functools.partial(lambda step, role: send_step(role, step), step))
        if step == 0:
            for k in range(3):
                act_copy(k).start()
        if step == 2:
            load_w.wait()
        if step == 3:
            for k in range(3):
                act_copy(k).wait()
            for k in range(4):
                act_t_out[:, k * 128:(k + 1) * 128] = av[k]
        if step >= 2:
            lump, chunk = (step - 2) // PIECES, (step - 2) % PIECES
            multiply_chunk(lump, chunk)
            if chunk == PIECES - 1:
                save_bins(lump)
                send_parts(lump)
    for chunk in (0, 2, 1, 3):
        multiply_chunk(3, chunk)
    save_bins(3)
    send_parts(3)
    for step in (STEPS, STEPS + 1):
        each_role(functools.partial(lambda step, role: send_step(role, step), step))
    totals = []
    for par in range(2):
        plane = 2 * lax.rem(c, 2) + par
        total = acc[plane, pl.ds(pl.multiple_of((c // 2) * 64, 64), 64), :]
        for k in range(3):
            pltpu.make_async_remote_copy(
                src_ref=parts.at[k, par], dst_ref=parts.at[k, par],
                send_sem=part_sent.at[0, 0], recv_sem=part_in.at[k, par],
                device_id=peers[k], device_id_type=MESH,
            ).wait_recv()
            total += parts[k, par]
        totals.append(total)
    din_out[...] = jnp.concatenate(totals, axis=0).T.astype(din_out.dtype)
    for plane in range(4):
        for xs in range(2):
            remote, copy = part_copy(plane, xs)
            pl.when(remote)(copy.wait_send)
            bin_copy(plane, xs).wait()


def weight_kernel(tiles, act_ref, g_ref, out_ref):
    per_step = g_ref.shape[1] // 256
    for k in range(per_step):
        @pl.when(pl.program_id(0) * per_step + k < tiles)
        def _():
            cols = slice(k * 256, (k + 1) * 256)
            out_ref[:, cols] = jnp.dot(
                act_ref[...], g_ref[:, cols], preferred_element_type=jnp.float32
            ).astype(out_ref.dtype)


def fused(activations, upstream, weight, bin_fill):
    d, ff = weight.shape
    tokens = upstream.shape[0] * 8
    vmem = pl.BlockSpec(memory_space=pltpu.VMEM)
    hbm = pl.BlockSpec(memory_space=pltpu.HBM)
    dma = pltpu.SemaphoreType.DMA
    bf16, f32 = jnp.bfloat16, jnp.float32
    gathered, act_t, d_input = pl.pallas_call(
        gather_kernel,
        out_shape=(
            jax.ShapeDtypeStruct((tokens, ff), bf16),
            jax.ShapeDtypeStruct((d, tokens), bf16),
            jax.ShapeDtypeStruct((d, 128), bf16),
        ),
        in_specs=[hbm, pl.BlockSpec(memory_space=pltpu.SMEM), vmem, hbm],
        out_specs=(hbm, vmem, vmem),
        scratch_shapes=[
            pltpu.VMEM((4, 128, ff), bf16),
            pltpu.VMEM((d, ff), bf16),
            pltpu.VMEM((64, ff), bf16),
            pltpu.VMEM((4, d, 128), bf16),
            pltpu.VMEM((4, 128, d), f32),
            pltpu.VMEM((3, 2, 64, d), f32),
            dma((4, 2 * PIECES)), dma((3, STEPS)), dma((3,)), dma((3,)),
            dma((3, 2)), dma((4, 2)), dma, dma, dma((4, 2)),
        ],
        compiler_params=pltpu.CompilerParams(
            collective_id=0, has_side_effects=True, vmem_limit_bytes=60 * 2**20
        ),
        cost_estimate=pl.CostEstimate(
            flops=2 * tokens * ff * d, bytes_accessed=2 * ff * (d + tokens), transcendentals=0
        ),
    )(upstream, bin_fill, activations.T, weight)
    tile = 1024
    d_weight = pl.pallas_call(
        functools.partial(weight_kernel, ff // 256),
        out_shape=jax.ShapeDtypeStruct((d, ff), bf16),
        grid=(pl.cdiv(ff, tile),),
        in_specs=[
            pl.BlockSpec((d, tokens), lambda i: (0, 0)),
            pl.BlockSpec((tokens, tile), lambda i: (0, i)),
        ],
        out_specs=pl.BlockSpec((d, tile), lambda i: (0, i)),
        compiler_params=pltpu.CompilerParams(vmem_limit_bytes=58 * 2**20),
        cost_estimate=pl.CostEstimate(
            flops=2 * tokens * ff * d, bytes_accessed=2 * ff * (d + tokens), transcendentals=0
        ),
    )(act_t, gathered)
    return d_input.T, d_weight


def plain(activations, upstream, weight, bin_fill):
    live_rows = jnp.arange(upstream.shape[0], dtype=jnp.int32) < bin_fill[0]
    masked = jnp.where(live_rows[:, None], upstream, jnp.zeros_like(upstream))
    all_inputs = lax.all_gather(activations, "col", axis=0, tiled=True)
    block_rows = lax.all_gather(masked, ("dp", "row"), axis=0, tiled=True)
    grad_w = lax.dot_general(
        all_inputs, block_rows, (((0,), (0,)), ((), ())), preferred_element_type=jnp.float32
    )
    grad_x = lax.dot_general(
        block_rows, weight, (((1,), (1,)), ((), ())), preferred_element_type=jnp.float32
    )
    d_input = lax.psum_scatter(grad_x, "col", scatter_dimension=0, tiled=True)
    return d_input.astype(jnp.bfloat16), grad_w.astype(jnp.bfloat16)


def solution(mesh):
    sizes = tuple(mesh.shape[name] for name in ("dp", "row", "col"))
    in_specs = (
        P("col", ("dp", "row")),
        P(("dp", "row"), "col"),
        P(("dp", "row"), "col"),
        P(("dp", "row")),
    )
    out_specs = (P("col", ("dp", "row")), P(("dp", "row"), "col"))
    return jax.shard_map(
        fused if sizes == (2, 4, 4) else plain,
        mesh=mesh, in_specs=in_specs, out_specs=out_specs, check_vma=False,
    )
```

```python
import functools

import jax
import jax.numpy as jnp
from jax import lax
from jax.experimental import pallas as pl
from jax.experimental.pallas import tpu as pltpu
from jax.sharding import PartitionSpec as P

MESH = pl.DeviceIdType.MESH
PIECES = 8
STEPS = 28
WINDOW = 3


ALL = tuple(range(PIECES))


def own(plane, order=ALL):
    return [(plane, 0, chunk) for chunk in order]


def other(plane, order=ALL):
    return [(plane, 1, chunk) for chunk in order]


END = {
    "x": own(0) + own(1) + own(2) + own(3, (0, 1, 2, 3)),
    "in": own(0) + other(0),
}
MIDDLE = {
    "x": own(1) + own(2) + own(3, (4, 5, 6, 7, 0, 1, 2, 3)),
    "in": own(1) + own(0),
    "out": own(1) + own(2) + own(3, (0, 1, 2, 3))
    + [(3, side, chunk) for chunk in (4, 5, 6, 7) for side in (0, 1)],
}
TAIL = (6, 2, 3, 7)
LAST = {23: 4, 25: 5, 26: 0, 27: 1}
LINKS = ("x", "in", "out")
ORDER = ((0, 1, 2, 3), (1, 0, 2, 3))


def weight_columns(act, g, out, low, high):
    def body(k, carry):
        cols = pl.ds(pl.multiple_of(k * 256, 256), 256)
        out[:, cols] = jnp.dot(
            act[...], g[:, :, cols].reshape(512, 256), preferred_element_type=jnp.float32
        ).astype(out.dtype)
        return carry

    lax.fori_loop(low, high, body, 0)


def gather_kernel(
    up_ref, fill_ref, act_ref, w_ref, dw_out, g_out, act_out, din_out,
    gv, wv, uv, av, act, dw, acc, parts, piece_in, piece_out, act_in, act_sent,
    part_in, part_sent, w_sem, up_sem, act_sem, save_sem,
):
    x, z, c = lax.axis_index("dp"), lax.axis_index("row"), lax.axis_index("col")
    side = z // 2
    is_end = (z == 0) | (z == 3)
    is_middle = (z == 1) | (z == 2)
    inward, outward = z + 1 - 2 * side, z - 1 + 2 * side
    targets = {"x": {"dp": 1 - x}, "in": {"row": inward}, "out": {"row": outward}}
    peers = [{"col": lax.rem(c + k, 4)} for k in (1, 2, 3)]
    ff = gv.shape[2]
    tiles = ff // 256
    cut = [tiles * i // PIECES for i in range(PIECES + 1)]

    def absolute(plane):
        return plane + side * (3 - 2 * plane)

    load_up = pltpu.make_async_copy(up_ref, uv, up_sem)
    load_up.start()
    load_w = pltpu.make_async_copy(w_ref, wv, w_sem)
    load_w.start()
    barrier = pltpu.get_barrier_semaphore()
    for target in [targets["x"], targets["in"]] + peers:
        pl.semaphore_signal(barrier, inc=1, device_id=target, device_id_type=MESH)

    @pl.when(is_middle)
    def _():
        pl.semaphore_signal(barrier, inc=1, device_id=targets["out"], device_id_type=MESH)

    av[c] = act_ref[...]
    load_up.wait()
    live = lax.broadcasted_iota(jnp.int32, uv.shape, 0) < fill_ref[0]
    here = pl.ds(pl.multiple_of(x * 64, 64), 64)
    gv[z, here, :] = jnp.where(live, uv[...], jnp.zeros_like(uv))

    @pl.when(is_middle)
    def _():
        pl.semaphore_wait(barrier, 6)

    @pl.when(is_end)
    def _():
        pl.semaphore_wait(barrier, 5)

    def piece_copy(piece, link, step):
        plane, from_other, chunk = piece
        xs = 1 - x if from_other else x
        rows = pl.ds(pl.multiple_of(xs * 64, 64), 64)
        low, high = cut[chunk] * 256, cut[chunk + 1] * 256
        ref = gv.at[absolute(plane), rows, low:high]
        return pltpu.make_async_remote_copy(
            src_ref=ref, dst_ref=ref,
            send_sem=piece_out.at[LINKS.index(link), step],
            recv_sem=piece_in.at[absolute(plane), xs * PIECES + chunk],
            device_id=targets[link], device_id_type=MESH,
        )

    arrived = [set(own(0)), set(own(1))]

    def need(role, piece):
        if piece not in arrived[role]:
            arrived[role].add(piece)
            piece_copy(piece, "x", 0).wait_recv()

    def send_step(role, step):
        queues = (END, MIDDLE)[role]
        for link, queue in queues.items():
            if WINDOW <= step < len(queue) + WINDOW:
                piece_copy(queue[step - WINDOW], link, step - WINDOW).wait_send()
            if step < len(queue):
                need(role, queue[step])
                piece_copy(queue[step], link, step).start()

    def each_role(do):
        pl.when(is_end)(lambda: do(0))
        pl.when(is_middle)(lambda: do(1))

    def lump_plane(lump):
        first, second = ORDER[0][lump], ORDER[1][lump]
        return absolute(jnp.where(is_end, first, second))

    def multiply_chunk(lump, chunk):
        def wait_chunk(role):
            plane = ORDER[role][lump]
            need(role, (plane, 0, chunk))
            need(role, (plane, 1, chunk))

        each_role(wait_chunk)
        multiply(lump, cut[chunk], cut[chunk + 1])

    def save(chunk):
        cols = slice(cut[chunk] * 256, cut[chunk + 1] * 256)
        if chunk in TAIL:
            src, dst = gv.at[:, :, cols], g_out.at[:, :, cols]
        else:
            src, dst = dw.at[:, cols], dw_out.at[:, cols]
        return pltpu.make_async_copy(src, dst, save_sem.at[chunk])

    save_act = pltpu.make_async_copy(act, act_out, act_sem)

    def multiply(lump, low, high):
        plane = lump_plane(lump)

        def body(k, carry):
            cols = pl.ds(pl.multiple_of(k * 256, 256), 256)
            acc[plane] += lax.dot_general(
                gv[plane, :, cols], wv[:, cols], (((1,), (1,)), ((), ())),
                preferred_element_type=jnp.float32,
            )
            return carry

        lax.fori_loop(low, high, body, 0)

    def part_copy(plane, xs):
        owner = xs * 2 + plane // 2
        apart = lax.rem(c - owner + 4, 4)
        slot = jnp.maximum(apart - 1, 0)
        copy = pltpu.make_async_remote_copy(
            src_ref=acc.at[plane, pl.ds(xs * 64, 64), :],
            dst_ref=parts.at[slot, lax.rem(plane, 2)],
            send_sem=part_sent.at[plane, xs],
            recv_sem=part_in.at[slot, lax.rem(plane, 2)],
            device_id={"col": owner}, device_id_type=MESH,
        )
        return apart != 0, copy

    def send_parts(lump):
        for xs in range(2):
            remote, copy = part_copy(lump_plane(lump), xs)
            pl.when(remote)(copy.start)

    def act_copy(k):
        return pltpu.make_async_remote_copy(
            src_ref=av.at[c], dst_ref=av.at[c],
            send_sem=act_sent.at[k], recv_sem=act_in.at[k],
            device_id=peers[k], device_id_type=MESH,
        )

    acc[...] = jnp.zeros_like(acc)
    for step in range(STEPS):
        each_role(functools.partial(lambda step, role: send_step(role, step), step))
        if step == 0:
            for k in range(3):
                act_copy(k).start()
        if step == 2:
            load_w.wait()
        if step == 3:
            for k in range(3):
                act_copy(k).wait()
            for plane in range(4):
                half = slice((plane % 2) * 64, (plane % 2) * 64 + 64)
                act[:, plane * 128:(plane + 1) * 128] = jnp.concatenate(
                    [av[plane // 2][:, half], av[2 + plane // 2][:, half]], axis=1
                )
            save_act.start()
        if 2 <= step < 2 + 3 * PIECES:
            lump, chunk = (step - 2) // PIECES, (step - 2) % PIECES
            multiply_chunk(lump, chunk)
            if chunk == PIECES - 1:
                send_parts(lump)
        if step in LAST:
            multiply_chunk(3, LAST[step])
            weight_columns(act, gv, dw, cut[LAST[step]], cut[LAST[step] + 1])
            save(LAST[step]).start()
    for chunk in TAIL:
        multiply_chunk(3, chunk)
        save(chunk).start()
    send_parts(3)
    for step in range(STEPS, STEPS + WINDOW):
        each_role(functools.partial(lambda step, role: send_step(role, step), step))
    totals = []
    for par in range(2):
        plane = 2 * lax.rem(c, 2) + par
        total = acc[plane, pl.ds(pl.multiple_of((c // 2) * 64, 64), 64), :]
        for k in range(3):
            pltpu.make_async_remote_copy(
                src_ref=parts.at[k, par], dst_ref=parts.at[k, par],
                send_sem=part_sent.at[0, 0], recv_sem=part_in.at[k, par],
                device_id=peers[k], device_id_type=MESH,
            ).wait_recv()
            total += parts[k, par]
        totals.append(total)
    din_out[...] = jnp.concatenate(totals, axis=0).T.astype(din_out.dtype)
    for plane in range(4):
        for xs in range(2):
            remote, copy = part_copy(plane, xs)
            pl.when(remote)(copy.wait_send)
    save_act.wait()
    for chunk in ALL:
        save(chunk).wait()


def weight_kernel(dw_ref, g_ref, act_ref, out_ref, act, gv, dw, act_sem, in_sem, out_sem):
    tiles = out_ref.shape[1] // 256
    cut = [tiles * i // PIECES for i in range(PIECES + 1)]
    columns = [slice(cut[i] * 256, cut[i + 1] * 256) for i in ALL]
    load_act = pltpu.make_async_copy(act_ref, act, act_sem)
    load_act.start()
    loads = {
        i: pltpu.make_async_copy(g_ref.at[:, :, columns[i]], gv.at[:, :, columns[i]], in_sem.at[i])
        for i in TAIL
    }
    for load in loads.values():
        load.start()
    saves = {
        i: pltpu.make_async_copy(
            (dw if i in TAIL else dw_ref).at[:, columns[i]], out_ref.at[:, columns[i]], out_sem.at[i]
        )
        for i in ALL
    }
    for i in ALL:
        if i not in TAIL:
            saves[i].start()
    load_act.wait()
    for i in TAIL:
        loads[i].wait()
        weight_columns(act, gv, dw, cut[i], cut[i + 1])
        saves[i].start()
    for i in ALL:
        saves[i].wait()


def fused(activations, upstream, weight, bin_fill):
    d, ff = weight.shape
    tokens = upstream.shape[0] * 8
    vmem = pl.BlockSpec(memory_space=pltpu.VMEM)
    hbm = pl.BlockSpec(memory_space=pltpu.HBM)
    dma = pltpu.SemaphoreType.DMA
    bf16, f32 = jnp.bfloat16, jnp.float32
    dw_head, gathered, act_t, d_input = pl.pallas_call(
        gather_kernel,
        out_shape=(
            jax.ShapeDtypeStruct((d, ff), bf16),
            jax.ShapeDtypeStruct((4, 128, ff), bf16),
            jax.ShapeDtypeStruct((d, tokens), bf16),
            jax.ShapeDtypeStruct((d, 128), bf16),
        ),
        in_specs=[hbm, pl.BlockSpec(memory_space=pltpu.SMEM), vmem, hbm],
        out_specs=(hbm, hbm, hbm, vmem),
        scratch_shapes=[
            pltpu.VMEM((4, 128, ff), bf16),
            pltpu.VMEM((d, ff), bf16),
            pltpu.VMEM((64, ff), bf16),
            pltpu.VMEM((4, d, 128), bf16),
            pltpu.VMEM((d, tokens), bf16),
            pltpu.VMEM((d, ff), bf16),
            pltpu.VMEM((4, 128, d), f32),
            pltpu.VMEM((3, 2, 64, d), f32),
            dma((4, 2 * PIECES)), dma((3, STEPS)), dma((3,)), dma((3,)),
            dma((3, 2)), dma((4, 2)), dma, dma, dma, dma((PIECES,)),
        ],
        compiler_params=pltpu.CompilerParams(
            collective_id=0, has_side_effects=True, vmem_limit_bytes=60 * 2**20
        ),
        cost_estimate=pl.CostEstimate(
            flops=4 * tokens * ff * d, bytes_accessed=4 * ff * d, transcendentals=0
        ),
    )(upstream, bin_fill, activations.T, weight)
    d_weight = pl.pallas_call(
        weight_kernel,
        out_shape=jax.ShapeDtypeStruct((d, ff), bf16),
        in_specs=[hbm] * 3,
        out_specs=hbm,
        scratch_shapes=[
            pltpu.VMEM((d, tokens), bf16),
            pltpu.VMEM((4, 128, ff), bf16),
            pltpu.VMEM((d, ff), bf16),
            dma, dma((PIECES,)), dma((PIECES,)),
        ],
        compiler_params=pltpu.CompilerParams(vmem_limit_bytes=60 * 2**20),
        cost_estimate=pl.CostEstimate(
            flops=tokens * ff * d, bytes_accessed=4 * ff * d, transcendentals=0
        ),
    )(dw_head, gathered, act_t)
    return d_input.T, d_weight


def plain(activations, upstream, weight, bin_fill):
    live_rows = jnp.arange(upstream.shape[0], dtype=jnp.int32) < bin_fill[0]
    masked = jnp.where(live_rows[:, None], upstream, jnp.zeros_like(upstream))
    all_inputs = lax.all_gather(activations, "col", axis=0, tiled=True)
    block_rows = lax.all_gather(masked, ("dp", "row"), axis=0, tiled=True)
    grad_w = lax.dot_general(
        all_inputs, block_rows, (((0,), (0,)), ((), ())), preferred_element_type=jnp.float32
    )
    grad_x = lax.dot_general(
        block_rows, weight, (((1,), (1,)), ((), ())), preferred_element_type=jnp.float32
    )
    d_input = lax.psum_scatter(grad_x, "col", scatter_dimension=0, tiled=True)
    return d_input.astype(jnp.bfloat16), grad_w.astype(jnp.bfloat16)


def solution(mesh):
    sizes = tuple(mesh.shape[name] for name in ("dp", "row", "col"))
    in_specs = (
        P("col", ("dp", "row")),
        P(("dp", "row"), "col"),
        P(("dp", "row"), "col"),
        P(("dp", "row")),
    )
    out_specs = (P("col", ("dp", "row")), P(("dp", "row"), "col"))
    return jax.shard_map(
        fused if sizes == (2, 4, 4) else plain,
        mesh=mesh, in_specs=in_specs, out_specs=out_specs, check_vma=False,
    )
```

```python
import functools

import jax
import jax.numpy as jnp
from jax import lax
from jax.experimental import pallas as pl
from jax.experimental.pallas import tpu as pltpu
from jax.sharding import PartitionSpec as P

MESH = pl.DeviceIdType.MESH
PIECES = 8
STEPS = 28
WINDOW = 3


ALL = tuple(range(PIECES))


def own(plane, order=ALL):
    return [(plane, 0, chunk) for chunk in order]


def other(plane, order=ALL):
    return [(plane, 1, chunk) for chunk in order]


END = {
    "x": own(0) + own(1) + own(2) + own(3, (0, 1, 2, 3)),
    "in": own(0) + other(0),
}
MIDDLE = {
    "x": own(1) + own(2) + own(3, (4, 5, 6, 7, 0, 1, 2, 3)),
    "in": own(1) + own(0),
    "out": own(1) + own(2) + own(3, (0, 1, 2, 3))
    + [(3, side, chunk) for chunk in (4, 5, 6, 7) for side in (0, 1)],
}
TAIL = (6, 2, 3, 7)
LAST = {23: 4, 25: 5, 26: 0, 27: 1}
LINKS = ("x", "in", "out")
ORDER = ((0, 1, 2, 3), (1, 0, 2, 3))


def weight_columns(act, g, out, low, high):
    def body(k, carry):
        cols = pl.ds(pl.multiple_of(k * 256, 256), 256)
        out[:, cols] = jnp.dot(
            act[...], g[:, :, cols].reshape(512, 256), preferred_element_type=jnp.float32
        ).astype(out.dtype)
        return carry

    lax.fori_loop(low, high, body, 0)


def gather_kernel(
    up_ref, fill_ref, act_ref, w_ref, dw_out, g_out, act_out, din_out,
    gv, wv, uv, av, act, dw, acc, parts, piece_in, piece_out, act_in, act_sent,
    part_in, part_sent, w_sem, up_sem, act_sem, save_sem,
):
    x, z, c = lax.axis_index("dp"), lax.axis_index("row"), lax.axis_index("col")
    side = z // 2
    is_end = (z == 0) | (z == 3)
    is_middle = (z == 1) | (z == 2)
    inward, outward = z + 1 - 2 * side, z - 1 + 2 * side
    targets = {"x": {"dp": 1 - x}, "in": {"row": inward}, "out": {"row": outward}}
    peers = [{"col": lax.rem(c + k, 4)} for k in (1, 2, 3)]
    ff = gv.shape[2]
    tiles = ff // 256
    cut = [tiles * i // PIECES for i in range(PIECES + 1)]

    def absolute(plane):
        return plane + side * (3 - 2 * plane)

    load_up = pltpu.make_async_copy(up_ref, uv, up_sem)
    load_up.start()
    load_w = pltpu.make_async_copy(w_ref, wv, w_sem)
    load_w.start()
    barrier = pltpu.get_barrier_semaphore()
    for target in [targets["x"], targets["in"]] + peers:
        pl.semaphore_signal(barrier, inc=1, device_id=target, device_id_type=MESH)

    @pl.when(is_middle)
    def _():
        pl.semaphore_signal(barrier, inc=1, device_id=targets["out"], device_id_type=MESH)

    av[c] = act_ref[...]
    load_up.wait()
    live = lax.broadcasted_iota(jnp.int32, uv.shape, 0) < fill_ref[0]
    here = pl.ds(pl.multiple_of(x * 64, 64), 64)
    gv[z, here, :] = jnp.where(live, uv[...], jnp.zeros_like(uv))

    @pl.when(is_middle)
    def _():
        pl.semaphore_wait(barrier, 6)

    @pl.when(is_end)
    def _():
        pl.semaphore_wait(barrier, 5)

    def piece_copy(piece, link, step):
        plane, from_other, chunk = piece
        xs = 1 - x if from_other else x
        rows = pl.ds(pl.multiple_of(xs * 64, 64), 64)
        low, high = cut[chunk] * 256, cut[chunk + 1] * 256
        ref = gv.at[absolute(plane), rows, low:high]
        return pltpu.make_async_remote_copy(
            src_ref=ref, dst_ref=ref,
            send_sem=piece_out.at[LINKS.index(link), step],
            recv_sem=piece_in.at[absolute(plane), xs * PIECES + chunk],
            device_id=targets[link], device_id_type=MESH,
        )

    arrived = [set(own(0)), set(own(1))]

    def need(role, piece):
        if piece not in arrived[role]:
            arrived[role].add(piece)
            piece_copy(piece, "x", 0).wait_recv()

    def send_step(role, step):
        queues = (END, MIDDLE)[role]
        for link, queue in queues.items():
            if WINDOW <= step < len(queue) + WINDOW:
                piece_copy(queue[step - WINDOW], link, step - WINDOW).wait_send()
            if step < len(queue):
                need(role, queue[step])
                piece_copy(queue[step], link, step).start()

    def each_role(do):
        pl.when(is_end)(lambda: do(0))
        pl.when(is_middle)(lambda: do(1))

    def lump_plane(lump):
        first, second = ORDER[0][lump], ORDER[1][lump]
        return absolute(jnp.where(is_end, first, second))

    def multiply_chunk(lump, chunk):
        def wait_chunk(role):
            plane = ORDER[role][lump]
            need(role, (plane, 0, chunk))
            need(role, (plane, 1, chunk))

        each_role(wait_chunk)
        multiply(lump, cut[chunk], cut[chunk + 1])

    def save(chunk):
        cols = slice(cut[chunk] * 256, cut[chunk + 1] * 256)
        if chunk in TAIL:
            src, dst = gv.at[:, :, cols], g_out.at[:, :, cols]
        else:
            src, dst = dw.at[:, cols], dw_out.at[:, cols]
        return pltpu.make_async_copy(src, dst, save_sem.at[chunk])

    save_act = pltpu.make_async_copy(act, act_out, act_sem)

    def multiply(lump, low, high):
        plane = lump_plane(lump)

        def body(k, carry):
            cols = pl.ds(pl.multiple_of(k * 256, 256), 256)
            acc[plane] += lax.dot_general(
                gv[plane, :, cols], wv[:, cols], (((1,), (1,)), ((), ())),
                preferred_element_type=jnp.float32,
            )
            return carry

        lax.fori_loop(low, high, body, 0)

    def part_copy(plane, xs):
        owner = xs * 2 + plane // 2
        apart = lax.rem(c - owner + 4, 4)
        slot = jnp.maximum(apart - 1, 0)
        copy = pltpu.make_async_remote_copy(
            src_ref=acc.at[plane, pl.ds(xs * 64, 64), :],
            dst_ref=parts.at[slot, lax.rem(plane, 2)],
            send_sem=part_sent.at[plane, xs],
            recv_sem=part_in.at[slot, lax.rem(plane, 2)],
            device_id={"col": owner}, device_id_type=MESH,
        )
        return apart != 0, copy

    def send_parts(lump):
        for xs in range(2):
            remote, copy = part_copy(lump_plane(lump), xs)
            pl.when(remote)(copy.start)

    def act_copy(k):
        return pltpu.make_async_remote_copy(
            src_ref=av.at[c], dst_ref=av.at[c],
            send_sem=act_sent.at[k], recv_sem=act_in.at[k],
            device_id=peers[k], device_id_type=MESH,
        )

    acc[...] = jnp.zeros_like(acc)
    for step in range(STEPS):
        each_role(functools.partial(lambda step, role: send_step(role, step), step))
        if step == 0:
            for k in range(3):
                act_copy(k).start()
        if step == 2:
            load_w.wait()
        if step == 3:
            for k in range(3):
                act_copy(k).wait()
            for plane in range(4):
                half = slice((plane % 2) * 64, (plane % 2) * 64 + 64)
                act[:, plane * 128:(plane + 1) * 128] = jnp.concatenate(
                    [av[plane // 2][:, half], av[2 + plane // 2][:, half]], axis=1
                )
            save_act.start()
        if 2 <= step < 2 + 3 * PIECES:
            lump, chunk = (step - 2) // PIECES, (step - 2) % PIECES
            multiply_chunk(lump, chunk)
            if chunk == PIECES - 1:
                send_parts(lump)
        if step in LAST:
            multiply_chunk(3, LAST[step])
            weight_columns(act, gv, dw, cut[LAST[step]], cut[LAST[step] + 1])
            save(LAST[step]).start()
    for chunk in TAIL:
        multiply_chunk(3, chunk)
        save(chunk).start()
    send_parts(3)
    for step in range(STEPS, STEPS + WINDOW):
        each_role(functools.partial(lambda step, role: send_step(role, step), step))
    totals = []
    for par in range(2):
        plane = 2 * lax.rem(c, 2) + par
        total = acc[plane, pl.ds(pl.multiple_of((c // 2) * 64, 64), 64), :]
        for k in range(3):
            pltpu.make_async_remote_copy(
                src_ref=parts.at[k, par], dst_ref=parts.at[k, par],
                send_sem=part_sent.at[0, 0], recv_sem=part_in.at[k, par],
                device_id=peers[k], device_id_type=MESH,
            ).wait_recv()
            total += parts[k, par]
        totals.append(total)
    din_out[...] = jnp.concatenate(totals, axis=0).T.astype(din_out.dtype)
    for plane in range(4):
        for xs in range(2):
            remote, copy = part_copy(plane, xs)
            pl.when(remote)(copy.wait_send)
    save_act.wait()
    for chunk in ALL:
        save(chunk).wait()


def weight_kernel(dw_ref, g_ref, act_ref, out_ref, act, gv, dw, act_sem, in_sem, out_sem):
    tiles = out_ref.shape[1] // 256
    cut = [tiles * i // PIECES for i in range(PIECES + 1)]
    columns = [slice(cut[i] * 256, cut[i + 1] * 256) for i in ALL]
    load_act = pltpu.make_async_copy(act_ref, act, act_sem)
    load_act.start()
    loads = {
        i: pltpu.make_async_copy(g_ref.at[:, :, columns[i]], gv.at[:, :, columns[i]], in_sem.at[i])
        for i in TAIL
    }
    head = [i for i in ALL if i not in TAIL]
    for i in head:
        loads[i] = pltpu.make_async_copy(
            dw_ref.at[:, columns[i]], dw.at[:, columns[i]], in_sem.at[i]
        )
    for load in loads.values():
        load.start()
    saves = {
        i: pltpu.make_async_copy(dw.at[:, columns[i]], out_ref.at[:, columns[i]], out_sem.at[i])
        for i in ALL
    }
    load_act.wait()
    for i, j in zip(TAIL, head):
        loads[i].wait()
        weight_columns(act, gv, dw, cut[i], cut[i + 1])
        saves[i].start()
        loads[j].wait()
        saves[j].start()
    for i in ALL:
        saves[i].wait()


def fused(activations, upstream, weight, bin_fill):
    d, ff = weight.shape
    tokens = upstream.shape[0] * 8
    vmem = pl.BlockSpec(memory_space=pltpu.VMEM)
    hbm = pl.BlockSpec(memory_space=pltpu.HBM)
    dma = pltpu.SemaphoreType.DMA
    bf16, f32 = jnp.bfloat16, jnp.float32
    dw_head, gathered, act_t, d_input = pl.pallas_call(
        gather_kernel,
        out_shape=(
            jax.ShapeDtypeStruct((d, ff), bf16),
            jax.ShapeDtypeStruct((4, 128, ff), bf16),
            jax.ShapeDtypeStruct((d, tokens), bf16),
            jax.ShapeDtypeStruct((d, 128), bf16),
        ),
        in_specs=[hbm, pl.BlockSpec(memory_space=pltpu.SMEM), vmem, hbm],
        out_specs=(hbm, hbm, hbm, vmem),
        scratch_shapes=[
            pltpu.VMEM((4, 128, ff), bf16),
            pltpu.VMEM((d, ff), bf16),
            pltpu.VMEM((64, ff), bf16),
            pltpu.VMEM((4, d, 128), bf16),
            pltpu.VMEM((d, tokens), bf16),
            pltpu.VMEM((d, ff), bf16),
            pltpu.VMEM((4, 128, d), f32),
            pltpu.VMEM((3, 2, 64, d), f32),
            dma((4, 2 * PIECES)), dma((3, STEPS)), dma((3,)), dma((3,)),
            dma((3, 2)), dma((4, 2)), dma, dma, dma, dma((PIECES,)),
        ],
        compiler_params=pltpu.CompilerParams(
            collective_id=0, has_side_effects=True, vmem_limit_bytes=60 * 2**20
        ),
        cost_estimate=pl.CostEstimate(
            flops=4 * tokens * ff * d, bytes_accessed=4 * ff * d, transcendentals=0
        ),
    )(upstream, bin_fill, activations.T, weight)
    d_weight = pl.pallas_call(
        weight_kernel,
        out_shape=jax.ShapeDtypeStruct((d, ff), bf16),
        in_specs=[hbm] * 3,
        out_specs=hbm,
        scratch_shapes=[
            pltpu.VMEM((d, tokens), bf16),
            pltpu.VMEM((4, 128, ff), bf16),
            pltpu.VMEM((d, ff), bf16),
            dma, dma((PIECES,)), dma((PIECES,)),
        ],
        compiler_params=pltpu.CompilerParams(vmem_limit_bytes=60 * 2**20),
        cost_estimate=pl.CostEstimate(
            flops=tokens * ff * d, bytes_accessed=4 * ff * d, transcendentals=0
        ),
    )(dw_head, gathered, act_t)
    return d_input.T, d_weight


def plain(activations, upstream, weight, bin_fill):
    live_rows = jnp.arange(upstream.shape[0], dtype=jnp.int32) < bin_fill[0]
    masked = jnp.where(live_rows[:, None], upstream, jnp.zeros_like(upstream))
    all_inputs = lax.all_gather(activations, "col", axis=0, tiled=True)
    block_rows = lax.all_gather(masked, ("dp", "row"), axis=0, tiled=True)
    grad_w = lax.dot_general(
        all_inputs, block_rows, (((0,), (0,)), ((), ())), preferred_element_type=jnp.float32
    )
    grad_x = lax.dot_general(
        block_rows, weight, (((1,), (1,)), ((), ())), preferred_element_type=jnp.float32
    )
    d_input = lax.psum_scatter(grad_x, "col", scatter_dimension=0, tiled=True)
    return d_input.astype(jnp.bfloat16), grad_w.astype(jnp.bfloat16)


def solution(mesh):
    sizes = tuple(mesh.shape[name] for name in ("dp", "row", "col"))
    in_specs = (
        P("col", ("dp", "row")),
        P(("dp", "row"), "col"),
        P(("dp", "row"), "col"),
        P(("dp", "row")),
    )
    out_specs = (P("col", ("dp", "row")), P(("dp", "row"), "col"))
    return jax.shard_map(
        fused if sizes == (2, 4, 4) else plain,
        mesh=mesh, in_specs=in_specs, out_specs=out_specs, check_vma=False,
    )
```

```python
import functools

import jax
import jax.numpy as jnp
from jax import lax
from jax.experimental import pallas as pl
from jax.experimental.pallas import tpu as pltpu
from jax.sharding import PartitionSpec as P

MESH = pl.DeviceIdType.MESH
PIECES = 8
STEPS = 28
WINDOW = 5


ALL = tuple(range(PIECES))


def own(plane, order=ALL):
    return [(plane, 0, chunk) for chunk in order]


def other(plane, order=ALL):
    return [(plane, 1, chunk) for chunk in order]


END = {
    "x": own(0) + own(1) + own(2) + own(3, (0, 1, 2, 3)),
    "in": own(0) + other(0),
}
MIDDLE = {
    "x": own(1) + own(2) + own(3, (4, 5, 6, 7, 0, 1, 2, 3)),
    "in": own(1) + own(0),
    "out": own(1) + own(2) + own(3, (0, 1, 2, 3))
    + [(3, side, chunk) for chunk in (4, 5, 6, 7) for side in (0, 1)],
}
TAIL = (6, 2, 3, 7)
LAST = {23: 4, 25: 5, 26: 0, 27: 1}
LINKS = ("x", "in", "out")
ORDER = ((0, 1, 2, 3), (1, 0, 2, 3))


def weight_columns(act, g, out, low, high):
    def body(k, carry):
        cols = pl.ds(pl.multiple_of(k * 256, 256), 256)
        out[:, cols] = jnp.dot(
            act[...], g[:, :, cols].reshape(512, 256), preferred_element_type=jnp.float32
        ).astype(out.dtype)
        return carry

    lax.fori_loop(low, high, body, 0)


def gather_kernel(
    up_ref, fill_ref, act_ref, w_ref, dw_out, g_out, act_out, din_out,
    gv, wv, uv, av, act, dw, acc, parts, piece_in, piece_out, act_in, act_sent,
    part_in, part_sent, w_sem, up_sem, act_sem, save_sem,
):
    x, z, c = lax.axis_index("dp"), lax.axis_index("row"), lax.axis_index("col")
    side = z // 2
    is_end = (z == 0) | (z == 3)
    is_middle = (z == 1) | (z == 2)
    inward, outward = z + 1 - 2 * side, z - 1 + 2 * side
    targets = {"x": {"dp": 1 - x}, "in": {"row": inward}, "out": {"row": outward}}
    peers = [{"col": lax.rem(c + k, 4)} for k in (1, 2, 3)]
    ff = gv.shape[2]
    tiles = ff // 256
    cut = [tiles * i // PIECES for i in range(PIECES + 1)]

    def absolute(plane):
        return plane + side * (3 - 2 * plane)

    load_up = pltpu.make_async_copy(up_ref, uv, up_sem)
    load_up.start()
    load_w = pltpu.make_async_copy(w_ref, wv, w_sem)
    load_w.start()
    barrier = pltpu.get_barrier_semaphore()
    for target in [targets["x"], targets["in"]] + peers:
        pl.semaphore_signal(barrier, inc=1, device_id=target, device_id_type=MESH)

    @pl.when(is_middle)
    def _():
        pl.semaphore_signal(barrier, inc=1, device_id=targets["out"], device_id_type=MESH)

    av[c] = act_ref[...]
    load_up.wait()
    live = lax.broadcasted_iota(jnp.int32, uv.shape, 0) < fill_ref[0]
    here = pl.ds(pl.multiple_of(x * 64, 64), 64)
    gv[z, here, :] = jnp.where(live, uv[...], jnp.zeros_like(uv))

    @pl.when(is_middle)
    def _():
        pl.semaphore_wait(barrier, 6)

    @pl.when(is_end)
    def _():
        pl.semaphore_wait(barrier, 5)

    def piece_copy(piece, link, step):
        plane, from_other, chunk = piece
        xs = 1 - x if from_other else x
        rows = pl.ds(pl.multiple_of(xs * 64, 64), 64)
        low, high = cut[chunk] * 256, cut[chunk + 1] * 256
        ref = gv.at[absolute(plane), rows, low:high]
        return pltpu.make_async_remote_copy(
            src_ref=ref, dst_ref=ref,
            send_sem=piece_out.at[LINKS.index(link), step],
            recv_sem=piece_in.at[absolute(plane), xs * PIECES + chunk],
            device_id=targets[link], device_id_type=MESH,
        )

    arrived = [set(own(0)), set(own(1))]

    def need(role, piece):
        if piece not in arrived[role]:
            arrived[role].add(piece)
            piece_copy(piece, "x", 0).wait_recv()

    def send_step(role, step):
        queues = (END, MIDDLE)[role]
        for link, queue in queues.items():
            if WINDOW <= step < len(queue) + WINDOW:
                piece_copy(queue[step - WINDOW], link, step - WINDOW).wait_send()
            if step < len(queue):
                need(role, queue[step])
                piece_copy(queue[step], link, step).start()

    def each_role(do):
        pl.when(is_end)(lambda: do(0))
        pl.when(is_middle)(lambda: do(1))

    def lump_plane(lump):
        first, second = ORDER[0][lump], ORDER[1][lump]
        return absolute(jnp.where(is_end, first, second))

    def multiply_chunk(lump, chunk):
        def wait_chunk(role):
            plane = ORDER[role][lump]
            need(role, (plane, 0, chunk))
            need(role, (plane, 1, chunk))

        each_role(wait_chunk)
        multiply(lump, cut[chunk], cut[chunk + 1])

    def save(chunk):
        cols = slice(cut[chunk] * 256, cut[chunk + 1] * 256)
        if chunk in TAIL:
            src, dst = gv.at[:, :, cols], g_out.at[:, :, cols]
        else:
            src, dst = dw.at[:, cols], dw_out.at[:, cols]
        return pltpu.make_async_copy(src, dst, save_sem.at[chunk])

    save_act = pltpu.make_async_copy(act, act_out, act_sem)

    def multiply(lump, low, high):
        plane = lump_plane(lump)

        def body(k, carry):
            cols = pl.ds(pl.multiple_of(k * 256, 256), 256)
            acc[plane] += lax.dot_general(
                gv[plane, :, cols], wv[:, cols], (((1,), (1,)), ((), ())),
                preferred_element_type=jnp.float32,
            )
            return carry

        lax.fori_loop(low, high, body, 0)

    def part_copy(plane, xs):
        owner = xs * 2 + plane // 2
        apart = lax.rem(c - owner + 4, 4)
        slot = jnp.maximum(apart - 1, 0)
        copy = pltpu.make_async_remote_copy(
            src_ref=acc.at[plane, pl.ds(xs * 64, 64), :],
            dst_ref=parts.at[slot, lax.rem(plane, 2)],
            send_sem=part_sent.at[plane, xs],
            recv_sem=part_in.at[slot, lax.rem(plane, 2)],
            device_id={"col": owner}, device_id_type=MESH,
        )
        return apart != 0, copy

    def send_parts(lump):
        for xs in range(2):
            remote, copy = part_copy(lump_plane(lump), xs)
            pl.when(remote)(copy.start)

    def act_copy(k):
        return pltpu.make_async_remote_copy(
            src_ref=av.at[c], dst_ref=av.at[c],
            send_sem=act_sent.at[k], recv_sem=act_in.at[k],
            device_id=peers[k], device_id_type=MESH,
        )

    acc[...] = jnp.zeros_like(acc)
    for step in range(STEPS):
        each_role(functools.partial(lambda step, role: send_step(role, step), step))
        if step == 0:
            for k in range(3):
                act_copy(k).start()
        if step == 2:
            load_w.wait()
        if step == 3:
            for k in range(3):
                act_copy(k).wait()
            for plane in range(4):
                half = slice((plane % 2) * 64, (plane % 2) * 64 + 64)
                act[:, plane * 128:(plane + 1) * 128] = jnp.concatenate(
                    [av[plane // 2][:, half], av[2 + plane // 2][:, half]], axis=1
                )
            save_act.start()
        if 2 <= step < 2 + 3 * PIECES:
            lump, chunk = (step - 2) // PIECES, (step - 2) % PIECES
            multiply_chunk(lump, chunk)
            if chunk == PIECES - 1:
                send_parts(lump)
        if step in LAST:
            multiply_chunk(3, LAST[step])
            weight_columns(act, gv, dw, cut[LAST[step]], cut[LAST[step] + 1])
            save(LAST[step]).start()
    for chunk in TAIL:
        multiply_chunk(3, chunk)
        save(chunk).start()
    send_parts(3)
    for step in range(STEPS, STEPS + WINDOW):
        each_role(functools.partial(lambda step, role: send_step(role, step), step))
    totals = []
    for par in range(2):
        plane = 2 * lax.rem(c, 2) + par
        total = acc[plane, pl.ds(pl.multiple_of((c // 2) * 64, 64), 64), :]
        for k in range(3):
            pltpu.make_async_remote_copy(
                src_ref=parts.at[k, par], dst_ref=parts.at[k, par],
                send_sem=part_sent.at[0, 0], recv_sem=part_in.at[k, par],
                device_id=peers[k], device_id_type=MESH,
            ).wait_recv()
            total += parts[k, par]
        totals.append(total)
    din_out[...] = jnp.concatenate(totals, axis=0).T.astype(din_out.dtype)
    for plane in range(4):
        for xs in range(2):
            remote, copy = part_copy(plane, xs)
            pl.when(remote)(copy.wait_send)
    save_act.wait()
    for chunk in ALL:
        save(chunk).wait()


def weight_kernel(dw_ref, g_ref, act_ref, out_ref, act, gv, dw, act_sem, in_sem, out_sem):
    tiles = out_ref.shape[1] // 256
    cut = [tiles * i // PIECES for i in range(PIECES + 1)]
    columns = [slice(cut[i] * 256, cut[i + 1] * 256) for i in ALL]
    load_act = pltpu.make_async_copy(act_ref, act, act_sem)
    load_act.start()
    loads = {
        i: pltpu.make_async_copy(g_ref.at[:, :, columns[i]], gv.at[:, :, columns[i]], in_sem.at[i])
        for i in TAIL
    }
    head = [i for i in ALL if i not in TAIL]
    for i in head:
        loads[i] = pltpu.make_async_copy(
            dw_ref.at[:, columns[i]], dw.at[:, columns[i]], in_sem.at[i]
        )
    for load in loads.values():
        load.start()
    saves = {
        i: pltpu.make_async_copy(dw.at[:, columns[i]], out_ref.at[:, columns[i]], out_sem.at[i])
        for i in ALL
    }
    load_act.wait()
    for i, j in zip(TAIL, head):
        loads[i].wait()
        weight_columns(act, gv, dw, cut[i], cut[i + 1])
        saves[i].start()
        loads[j].wait()
        saves[j].start()
    for i in ALL:
        saves[i].wait()


def fused(activations, upstream, weight, bin_fill):
    d, ff = weight.shape
    tokens = upstream.shape[0] * 8
    vmem = pl.BlockSpec(memory_space=pltpu.VMEM)
    hbm = pl.BlockSpec(memory_space=pltpu.HBM)
    dma = pltpu.SemaphoreType.DMA
    bf16, f32 = jnp.bfloat16, jnp.float32
    dw_head, gathered, act_t, d_input = pl.pallas_call(
        gather_kernel,
        out_shape=(
            jax.ShapeDtypeStruct((d, ff), bf16),
            jax.ShapeDtypeStruct((4, 128, ff), bf16),
            jax.ShapeDtypeStruct((d, tokens), bf16),
            jax.ShapeDtypeStruct((d, 128), bf16),
        ),
        in_specs=[hbm, pl.BlockSpec(memory_space=pltpu.SMEM), vmem, hbm],
        out_specs=(hbm, hbm, hbm, vmem),
        scratch_shapes=[
            pltpu.VMEM((4, 128, ff), bf16),
            pltpu.VMEM((d, ff), bf16),
            pltpu.VMEM((64, ff), bf16),
            pltpu.VMEM((4, d, 128), bf16),
            pltpu.VMEM((d, tokens), bf16),
            pltpu.VMEM((d, ff), bf16),
            pltpu.VMEM((4, 128, d), f32),
            pltpu.VMEM((3, 2, 64, d), f32),
            dma((4, 2 * PIECES)), dma((3, STEPS)), dma((3,)), dma((3,)),
            dma((3, 2)), dma((4, 2)), dma, dma, dma, dma((PIECES,)),
        ],
        compiler_params=pltpu.CompilerParams(
            collective_id=0, has_side_effects=True, vmem_limit_bytes=60 * 2**20
        ),
        cost_estimate=pl.CostEstimate(
            flops=4 * tokens * ff * d, bytes_accessed=4 * ff * d, transcendentals=0
        ),
    )(upstream, bin_fill, activations.T, weight)
    d_weight = pl.pallas_call(
        weight_kernel,
        out_shape=jax.ShapeDtypeStruct((d, ff), bf16),
        in_specs=[hbm] * 3,
        out_specs=hbm,
        scratch_shapes=[
            pltpu.VMEM((d, tokens), bf16),
            pltpu.VMEM((4, 128, ff), bf16),
            pltpu.VMEM((d, ff), bf16),
            dma, dma((PIECES,)), dma((PIECES,)),
        ],
        compiler_params=pltpu.CompilerParams(vmem_limit_bytes=60 * 2**20),
        cost_estimate=pl.CostEstimate(
            flops=tokens * ff * d, bytes_accessed=4 * ff * d, transcendentals=0
        ),
    )(dw_head, gathered, act_t)
    return d_input.T, d_weight


def plain(activations, upstream, weight, bin_fill):
    live_rows = jnp.arange(upstream.shape[0], dtype=jnp.int32) < bin_fill[0]
    masked = jnp.where(live_rows[:, None], upstream, jnp.zeros_like(upstream))
    all_inputs = lax.all_gather(activations, "col", axis=0, tiled=True)
    block_rows = lax.all_gather(masked, ("dp", "row"), axis=0, tiled=True)
    grad_w = lax.dot_general(
        all_inputs, block_rows, (((0,), (0,)), ((), ())), preferred_element_type=jnp.float32
    )
    grad_x = lax.dot_general(
        block_rows, weight, (((1,), (1,)), ((), ())), preferred_element_type=jnp.float32
    )
    d_input = lax.psum_scatter(grad_x, "col", scatter_dimension=0, tiled=True)
    return d_input.astype(jnp.bfloat16), grad_w.astype(jnp.bfloat16)


def solution(mesh):
    sizes = tuple(mesh.shape[name] for name in ("dp", "row", "col"))
    in_specs = (
        P("col", ("dp", "row")),
        P(("dp", "row"), "col"),
        P(("dp", "row"), "col"),
        P(("dp", "row")),
    )
    out_specs = (P("col", ("dp", "row")), P(("dp", "row"), "col"))
    return jax.shard_map(
        fused if sizes == (2, 4, 4) else plain,
        mesh=mesh, in_specs=in_specs, out_specs=out_specs, check_vma=False,
    )
```
